256 devices in a mesh: row: 16 (over z_lo, x, core), col: 16 (over z_hi, y).
Axes of the slice: x: 4, y: 4, z: 8 (z_hi: 4, z_lo: 2; z = z_hi * 2 + z_lo), core: 2. Of those that a mesh axis runs over, the one named last changes fastest.
Arguments:
- amplitudes: float32 [2048, 4096], P('row', 'col'), may hold values from -6 to 6
- integrals: float32 [4096, 32768], P('row', 'col'), may hold values from -0.25 to 0.25
- amp_mask: int32 [32, 64], replicated, may hold values from 0 to 1, as said below
- int_mask: int32 [64, 512], P('row', 'col'), may hold values from 0 to 1, as said below
- res_mask: int32 [32, 512], P(None, 'col'), may hold values from 0 to 1, as said below
Outputs:
- residual: float32 [2048, 32768], P('row', 'col')
The draws below stay inside these ranges and needn't reach their ends.
Inputs may be any that keep to these rules, and one draw needn't show every extreme that they name: `amp_mask`: 1 marks a tile that is kept; any pattern of tiles may occur. `int_mask`: 1 marks a tile that is kept; any pattern of tiles may occur. `res_mask`: 1 marks a tile that is kept; any pattern of tiles may occur.
All inputs are finite; a program needn't handle non-finite values.
Results may differ from the reference program's by a relative error of at most 0.000076.
Values sent between devices are 32-bit elements; how exact they have to be, the bound alone decides.
A program may use at most 192 MiB of HBM per device.

```python
import jax
import jax.numpy as jnp
from jax import lax

TILE = 64
IJ_DEV = 128
CD_DEV = 256
AB_DEV = 2048
IJ = 2048
CD = 4096
AB = 32768


def tiles_with_block(key, rows, cols, block_rows, block_cols, ones_num, ones_den):
    base_key = jax.random.fold_in(key, 11)
    row_key = jax.random.fold_in(key, 12)
    col_key = jax.random.fold_in(key, 13)
    base = jax.random.randint(base_key, (rows, cols), 0, ones_den) < ones_num
    pick_row = jax.random.randint(row_key, (), 0, rows // block_rows)
    pick_col = jax.random.randint(col_key, (), 0, cols // block_cols)
    in_rows = jnp.arange(rows, dtype=jnp.int32) // block_rows == pick_row
    in_cols = jnp.arange(cols, dtype=jnp.int32) // block_cols == pick_col
    dense = in_rows[:, None] & in_cols[None, :]
    return (base | dense).astype(jnp.int32)


def draw_amp_mask(key, part):
    key = jax.random.fold_in(key, 1)
    block_rows = max(IJ_DEV // TILE, 1)
    return tiles_with_block(key, IJ // TILE, CD // TILE, block_rows, CD // TILE, 1, 2)


def draw_int_mask(key, part):
    key = jax.random.fold_in(key, 2)
    return tiles_with_block(key, CD // TILE, AB // TILE, CD_DEV // TILE, AB_DEV // TILE, 1, 4)


def draw_res_mask(key, part):
    key = jax.random.fold_in(key, 3)
    return tiles_with_block(key, IJ // TILE, AB // TILE, IJ // TILE, AB_DEV // TILE, 1, 2)


def steps_of(own_key, extent, shards, least, high):
    gain = 1.0
    for dim, shards_of in shards:
        steps = jax.random.uniform(jax.random.fold_in(jax.random.fold_in(own_key, 6), dim), (shards_of,), jnp.float32, least / len(shards), high / len(shards))
        gain = gain * jnp.repeat(jnp.exp(steps), extent[dim] // shards_of).reshape((-1,) + (1,) * (len(extent) - 1 - dim))
    return gain


def scatter_about(key, dims, deviation, reach, cuts=(), held_as=jnp.bfloat16):
    entries = deviation * jax.random.normal(key, dims, jnp.float32)
    if cuts:
        entries = entries * steps_of(key, dims, cuts, -0.22, 0.18)
    return jnp.clip(entries, -reach, reach).astype(held_as)


def setup_inputs(seed: int = 0) -> dict:
    seeds = jax.random.split(jax.random.key(seed), 6)
    return {
        "amplitudes": scatter_about(seeds[0], (IJ, CD), 1.0, 6.0, ((0, 16), (1, 16)), jnp.float32),
        "integrals": scatter_about(seeds[1], (CD, AB), (CD // 8) ** -0.5, 0.25, ((0, 16), (1, 16)), jnp.float32),
        "amp_mask": draw_amp_mask(jax.random.fold_in(seeds[5], 71), 0),
        "int_mask": draw_int_mask(jax.random.fold_in(seeds[5], 71), 0),
        "res_mask": draw_res_mask(jax.random.fold_in(seeds[5], 71), 0),
    }


def spread(values, tiles):
    rows = tiles.shape[0]
    cols = tiles.shape[1]
    shaped = values.reshape(rows, TILE, cols, TILE)
    return (shaped * tiles.astype(jnp.float32)[:, None, :, None]).reshape(values.shape)


def reference(amplitudes, integrals, amp_mask, int_mask, res_mask):
    sparse_amp = spread(amplitudes, amp_mask)
    sparse_int = spread(integrals, int_mask)
    product = jnp.dot(sparse_amp, sparse_int, preferred_element_type=jnp.float32, precision=lax.Precision.HIGHEST)
    return spread(product, res_mask)
```

```python
import jax
import jax.numpy as jnp
from jax import lax
from jax.experimental import pallas as pl
from jax.experimental.pallas import tpu as pltpu
from jax.sharding import PartitionSpec as P

TILE = 64
W = 256
HALF = 128
BACKLOG = 3
OWN, NEAR_Z, NEAR_X, FAR = 0, 1, 2, 3
MESH = pl.DeviceIdType.MESH
F32 = jnp.float32
BF16 = jnp.bfloat16


def device(x, z_lo, core, z_hi, y):
    return (z_lo * 8 + x * 2 + core, z_hi * 4 + y)


def remote(src, dst, send_sem, recv_sem, target):
    return pltpu.make_async_remote_copy(
        src_ref=src, dst_ref=dst, send_sem=send_sem, recv_sem=recv_sem,
        device_id=target, device_id_type=MESH,
    )


def onehot(shape, dim, offset):
    tile = lax.div(lax.broadcasted_iota(jnp.int32, shape, dim), TILE) + offset
    return (tile == lax.broadcasted_iota(jnp.int32, shape, 1 - dim)).astype(BF16)


def mm(a, b):
    return jnp.dot(a, b, preferred_element_type=F32)


def split(value):
    high = value.astype(BF16)
    return high, (value - high.astype(F32)).astype(BF16)


def kernel(
    amp_ref, int_ref, amp_mask_ref, int_mask_ref, res_mask_ref, out_ref,
    am, af, ah, al, bf, bh, bl, part, r1x, r1z, r2x, r2z, res_tiles, mask8,
    sa1, ra1, sa2, ra2, sb, rb, ss, rs, sf, rf, s1x, q1x, s1z, q1z, s2x, q2x, s2z, q2z,
):
    n = bf.shape[1]
    row, col = lax.axis_index("row"), lax.axis_index("col")
    core, x, z = lax.rem(row, 2), lax.rem(lax.div(row, 2), 4), lax.div(row, 8)
    y, h = lax.rem(col, 4), lax.div(col, 4)
    odd = lax.rem(x, 2)
    xa = x + 1 - 2 * odd
    xb = lax.rem(x + 3 + 2 * odd, 4)
    sib = device(x, z, 1 - core, h, y)
    dev_a = device(xa, z, core, h, y)
    dev_b = device(xb, z, core, h, y)
    dev_z = device(x, 1 - z, core, h, y)
    dev_y = [device(x, z, core, h, lax.rem(y + d, 4)) for d in (1, 2, 3)]
    kk = 2 * odd + core
    kk_sib = 2 * odd + 1 - core
    kk_a = 2 * (1 - odd) + core
    kk_as = 2 * (1 - odd) + 1 - core

    far_x = lax.rem(lax.rem(h, 2) + lax.div(x, 2), 2)
    to_x = x + far_x * (xb - x)
    to_z = lax.div(h, 2)
    far_z = lax.rem(to_z + z, 2)
    slot = 2 * far_x + far_z
    stays = slot == 0
    dev_h = [device(to_x, to_z, core, lax.rem(h + d, 4), y) for d in range(4)]
    from_h = 2 * z + lax.div(x, 2)
    sources = [
        (device(sx, sz, core, from_h, y), i)
        for i, (sx, sz) in enumerate(((x, z), (x, 1 - z), (xb, z), (xb, 1 - z)))
    ]
    hosts_self = from_h == h

    barrier = pltpu.get_barrier_semaphore()
    for peer in (sib, dev_a, dev_b, dev_z, *dev_y):
        pl.semaphore_signal(barrier, inc=1, device_id=peer, device_id_type=MESH)
    for peer, i in sources:
        if i == 0:
            @pl.when(jnp.logical_not(hosts_self))
            def _():
                pl.semaphore_signal(barrier, inc=1, device_id=peer, device_id_type=MESH)
        else:
            pl.semaphore_signal(barrier, inc=1, device_id=peer, device_id_type=MESH)

    rows = mm(onehot((2 * TILE, 32), 0, 2 * row), amp_mask_ref[...].astype(BF16)).astype(BF16)
    am[...] = amp_ref[...] * mm(rows, onehot((64, W), 1, 4 * col))
    mask8[...] = jnp.zeros_like(mask8)
    mask8[0:4, :] = int_mask_ref[...].astype(F32)

    pl.semaphore_wait(barrier, 11 - stays.astype(jnp.int32))

    def leg1(d):
        return remote(am, af.at[slot, y], sa1.at[d], ra1.at[slot], dev_h[d])

    @pl.when(stays)
    def _():
        pltpu.make_async_copy(am, af.at[slot, y], ra1.at[slot]).start()

    @pl.when(jnp.logical_not(stays))
    def _():
        leg1(0).start()

    for d in (1, 3, 2):
        leg1(d).start()

    def to_a(j):
        return remote(bf.at[kk, j], bf.at[kk, j], sb.at[j], rb.at[j], dev_a)

    def to_sib(j):
        return remote(bf.at[kk, j], bf.at[kk, j], ss.at[j], rs.at[j], sib)

    def forward(j):
        return remote(bf.at[kk_a, j], bf.at[kk_a, j], sf.at[j], rf.at[j], sib)

    mask8b = mask8[...].astype(BF16)
    for j in range(n):
        tiles = mm(mask8b, onehot((32, W), 1, (W // TILE) * j))
        for t in range(4):
            r = slice(t * TILE, (t + 1) * TILE)
            bf[kk, j, r, :] = int_ref[r, j * W:(j + 1) * W] * tiles[t:t + 1, :]
        to_a(j).start()
        to_sib(j).start()

    def leg2(s, d):
        return remote(af.at[s, y], af.at[s, y], sa2.at[s, d], ra2.at[s, d], dev_y[d])

    for s in (FAR, NEAR_X, NEAR_Z, OWN):
        remote(am, af.at[s, y], sa1.at[0], ra1.at[s], sib).wait_recv()
        for d in (0, 2, 1):
            leg2(s, d).start()

    res_rows = mm(onehot((2 * TILE, 32), 0, 2 * row), res_mask_ref[...].astype(BF16))
    res_tiles[...] = res_rows.astype(BF16)

    def take_amp(s):
        for d in range(3):
            leg2(s, d).wait_recv()
        for q in range(4):
            c = slice(q * W, (q + 1) * W)
            ah[s, :, c], al[s, :, c] = split(af[s, q])

    def take_int(j):
        remote(bf.at[kk_a, j], bf.at[kk_a, j], sb.at[j], rb.at[j], sib).wait_recv()
        forward(j).start()
        remote(bf.at[kk_sib, j], bf.at[kk_sib, j], ss.at[j], rs.at[j], sib).wait_recv()
        remote(bf.at[kk_as, j], bf.at[kk_as, j], sf.at[j], rf.at[j], sib).wait_recv()
        for q in range(4):
            r = slice(q * W, (q + 1) * W)
            bh[j, r, :], bl[j, r, :] = split(bf[q, j])

    def multiply(s, j):
        high = bh[j]
        total = mm(ah[s], high) + mm(al[s], high) + mm(ah[s], bl[j])
        part[s, j, 0] = total[:, :HALF]
        part[s, j, 1] = total[:, HALF:]

    def first_x(i, j):
        return remote(part.at[FAR - i, j, 0], r1x.at[j, i], s1x.at[j, i], q1x.at[j, i], dev_b)

    def first_z(i, j):
        s = FAR - 2 * i
        return remote(part.at[s, j, 1], r1z.at[j, i], s1z.at[j, i], q1z.at[j, i], dev_z)

    def second_z(j):
        return remote(part.at[NEAR_Z, j, 0], r2z.at[j], s2z.at[j], q2z.at[j], dev_z)

    def second_x(j):
        return remote(part.at[NEAR_X, j, 1], r2x.at[j], s2x.at[j], q2x.at[j], dev_b)

    def far(j):
        multiply(FAR, j)
        first_x(0, j).start()
        first_z(0, j).start()

    def near(j):
        multiply(NEAR_X, j)
        first_x(1, j).start()
        multiply(NEAR_Z, j)
        first_z(1, j).start()

    def second(j):
        first_x(0, j).wait_recv()
        part[NEAR_Z, j, 0] += r1x[j, 0]
        second_z(j).start()
        first_z(0, j).wait_recv()
        part[NEAR_X, j, 1] += r1z[j, 0]
        second_x(j).start()

    def loop(lo, hi, *steps):
        def body(j, carry):
            for step in steps:
                step(j)
            return carry

        lax.fori_loop(lo, hi, body, 0)

    take_amp(FAR)
    loop(0, BACKLOG, take_int, far)
    take_amp(NEAR_X)
    take_amp(NEAR_Z)
    loop(0, BACKLOG, near)
    loop(BACKLOG, n, take_int, far, near, lambda j: second(j - BACKLOG))
    take_amp(OWN)
    loop(0, n - BACKLOG, lambda j: multiply(OWN, j))
    loop(n - BACKLOG, n, second, lambda j: multiply(OWN, j))

    def finish(j):
        tiles = mm(res_tiles[...], onehot((32, W), 1, (W // TILE) * j))
        first_x(1, j).wait_recv()
        second_z(j).wait_recv()
        first_z(1, j).wait_recv()
        second_x(j).wait_recv()
        c = pl.multiple_of(j * W, W)
        left = part[OWN, j, 0] + r1x[j, 1] + r2z[j]
        right = part[OWN, j, 1] + r1z[j, 1] + r2x[j]
        out_ref[:, pl.ds(c, HALF)] = left * tiles[:, :HALF]
        out_ref[:, pl.ds(c + HALF, HALF)] = right * tiles[:, HALF:]

    loop(0, n, finish)

    @pl.when(jnp.logical_not(stays))
    def _():
        leg1(0).wait_send()

    for d in (1, 2, 3):
        leg1(d).wait_send()
    for s in range(4):
        for d in range(3):
            leg2(s, d).wait_send()

    def drain(j):
        to_a(j).wait_send()
        to_sib(j).wait_send()
        forward(j).wait_send()
        for i in range(2):
            first_x(i, j).wait_send()
            first_z(i, j).wait_send()
        second_x(j).wait_send()
        second_z(j).wait_send()

    loop(0, n, drain)


def on_device(amplitudes, integrals, amp_mask, int_mask, res_mask):
    rows, depth = amplitudes.shape
    cols = integrals.shape[1]
    n = cols // W
    dma = pltpu.SemaphoreType.DMA
    vmem = pltpu.VMEM
    return pl.pallas_call(
        kernel,
        out_shape=jax.ShapeDtypeStruct((rows, cols), F32),
        in_specs=[pl.BlockSpec(memory_space=pltpu.VMEM)] * 5,
        out_specs=pl.BlockSpec(memory_space=pltpu.VMEM),
        scratch_shapes=[
            vmem((rows, depth), F32),
            vmem((4, 4, rows, depth), F32),
            vmem((4, rows, 4 * depth), BF16),
            vmem((4, rows, 4 * depth), BF16),
            vmem((4, n, depth, W), F32),
            vmem((n, 4 * depth, W), BF16),
            vmem((n, 4 * depth, W), BF16),
            vmem((4, n, 2, rows, HALF), F32),
            vmem((n, 2, rows, HALF), F32),
            vmem((n, 2, rows, HALF), F32),
            vmem((n, rows, HALF), F32),
            vmem((n, rows, HALF), F32),
            vmem((rows, 32), BF16),
            vmem((8, 32), F32),
            dma((4,)), dma((4,)), dma((4, 3)), dma((4, 3)),
            dma((n,)), dma((n,)), dma((n,)), dma((n,)), dma((n,)), dma((n,)),
            dma((n, 2)), dma((n, 2)), dma((n, 2)), dma((n, 2)),
            dma((n,)), dma((n,)), dma((n,)), dma((n,)),
        ],
        compiler_params=pltpu.CompilerParams(
            collective_id=0, has_side_effects=True, vmem_limit_bytes=48 * 2**20
        ),
        cost_estimate=pl.CostEstimate(
            flops=2 * 3 * 4 * rows * 4 * depth * cols,
            bytes_accessed=4 * (rows * depth + depth * cols + rows * cols),
            transcendentals=0,
        ),
        name="ladder",
    )(amplitudes, integrals, amp_mask, int_mask, res_mask)


def solution(mesh):
    placed = (P("row", "col"), P("row", "col"), P(), P("row", "col"), P(None, "col"))
    return jax.shard_map(
        on_device, mesh=mesh, in_specs=placed, out_specs=P("row", "col"), check_vma=False
    )
```

```python
import jax
import jax.numpy as jnp
from jax import lax
from jax.experimental import pallas as pl
from jax.experimental.pallas import tpu as pltpu
from jax.sharding import PartitionSpec as P

TILE = 64
W = 256
HALF = 128
BACKLOG = 1
LAG = 2
EARLY = 4
OWN, NEAR_X, NEAR_Z, FAR = 0, 1, 2, 3
MESH = pl.DeviceIdType.MESH
F32 = jnp.float32
BF16 = jnp.bfloat16


def device(x, z_lo, core, z_hi, y):
    return (z_lo * 8 + x * 2 + core, z_hi * 4 + y)


def remote(src, dst, send_sem, recv_sem, target):
    return pltpu.make_async_remote_copy(
        src_ref=src, dst_ref=dst, send_sem=send_sem, recv_sem=recv_sem,
        device_id=target, device_id_type=MESH,
    )


def onehot(shape, dim, offset):
    tile = lax.div(lax.broadcasted_iota(jnp.int32, shape, dim), TILE) + offset
    return (tile == lax.broadcasted_iota(jnp.int32, shape, 1 - dim)).astype(BF16)


def mm(a, b):
    return jnp.dot(a, b, preferred_element_type=F32)


def split(value):
    high = value.astype(BF16)
    return high, (value - high.astype(F32)).astype(BF16)


def kernel(
    amp_hbm, int_hbm, amp_mask_hbm, int_mask_hbm, res_mask_hbm, out_ref,
    amp_in, int_in, amp_tiles, int_tiles, res_in,
    out_v, st, af, ah, al, bf, bh, bl, part, r1x, r1z, r2x, r2z, res_tiles, mask8,
    s_in, s_out, s0, q0, s1, q1, sf1, s2, q2, sf2, qf2,
    sb, rb, ss, rs, sf, rf, s1x, q1x, s1z, q1z, s2x, q2x, s2z, q2z,
):
    n = bf.shape[1]
    loads = [
        pltpu.make_async_copy(src, dst, s_in.at[i])
        for i, (src, dst) in enumerate((
            (amp_hbm, amp_in), (amp_mask_hbm, amp_tiles), (int_mask_hbm, int_tiles),
            (int_hbm, int_in), (res_mask_hbm, res_in),
        ))
    ]
    for load in loads:
        load.start()

    row, col = lax.axis_index("row"), lax.axis_index("col")
    core, x, z = lax.rem(row, 2), lax.rem(lax.div(row, 2), 4), lax.div(row, 8)
    y, h = lax.rem(col, 4), lax.div(col, 4)
    odd = lax.rem(x, 2)
    xa = x + 1 - 2 * odd
    xb = lax.rem(x + 3 + 2 * odd, 4)
    sib = device(x, z, 1 - core, h, y)
    dev_a = device(xa, z, core, h, y)
    dev_b = device(xb, z, core, h, y)
    dev_z = device(x, 1 - z, core, h, y)
    y_up, y_down = lax.rem(y + 1, 4), lax.rem(y + 3, 4)
    dev_y = (device(x, z, core, h, y_up), device(x, z, core, h, y_down))
    kk = 2 * odd + core
    kk_sib = 2 * odd + 1 - core
    kk_a = 2 * (1 - odd) + core
    kk_as = 2 * (1 - odd) + 1 - core

    def at(z_to, h_to):
        return device(x, z_to, core, lax.rem(h_to + 8, 4), y)

    def flag(condition):
        return condition.astype(jnp.int32)

    q = lax.div(x, 2)
    is_source = lax.rem(h, 2) == q
    z_to = lax.div(h, 2)
    offset = lax.rem(z + z_to, 2)
    targets = (
        at(z_to, h + 1 - offset),
        at(z_to, h - (1 - offset) + offset * (1 - 2 * z_to)),
    )
    h_from = 2 * z + q
    place = lax.rem(h - h_from + 4, 4)
    home = place == 0
    relay = 3 - 2 * q
    side = 1 + 2 * z
    relays = (place == relay, jnp.logical_or(home, place == side))
    relay_to = (at(z, h_from + 2), at(z, h_from + 2 + flag(home) * (1 - 2 * z)))
    opposite = place == 2
    from_aligned = at(z, h_from + relay * flag(opposite))
    direct = flag(jnp.logical_or(home, place == side))
    from_offset = at(z + direct * (1 - 2 * z), h_from + side * flag(opposite))

    barrier = pltpu.get_barrier_semaphore()
    for peer in (sib, dev_a, dev_b, dev_z, *dev_y, from_offset):
        pl.semaphore_signal(barrier, inc=1, device_id=peer, device_id_type=MESH)

    @pl.when(jnp.logical_not(home))
    def _():
        pl.semaphore_signal(barrier, inc=1, device_id=from_aligned, device_id_type=MESH)

    for load in loads[:2]:
        load.wait()
    rows = mm(onehot((2 * TILE, 32), 0, 2 * row), amp_tiles[...].astype(BF16)).astype(BF16)
    st[0] = amp_in[...] * mm(rows, onehot((64, W), 1, 4 * col))

    def to_a(j):
        return remote(bf.at[kk, j], bf.at[kk, j], sb.at[j], rb.at[j], dev_a)

    def to_sib(j):
        return remote(bf.at[kk, j], bf.at[kk, j], ss.at[j], rs.at[j], sib)

    def forward(j):
        return remote(bf.at[kk_a, j], bf.at[kk_a, j], sf.at[j], rf.at[j], sib)

    for load in loads[2:4]:
        load.wait()
    mask8[...] = jnp.zeros_like(mask8)
    mask8[0:4, :] = int_tiles[...].astype(F32)
    mask8b = mask8[...].astype(BF16)

    def mask_int(j):
        tiles = mm(mask8b, onehot((32, W), 1, (W // TILE) * j))
        for t in range(4):
            r = slice(t * TILE, (t + 1) * TILE)
            bf[kk, j, r, :] = int_in[r, j * W:(j + 1) * W] * tiles[t:t + 1, :]

    for j in range(EARLY):
        mask_int(j)

    pl.semaphore_wait(barrier, 6 + 2 * flag(is_source) + flag(relays[0]) + flag(relays[1]))

    def half(p):
        return pl.ds(p * TILE, TILE)

    def leg0(p):
        return remote(st.at[0, half(p)], st.at[1, half(p)], s0.at[p], q0.at[p], dev_b)

    def leg1(b, i, p):
        s = 2 * offset + b
        return remote(
            st.at[b, half(p)], af.at[s, y, half(p)], s1.at[b, i, p], q1.at[s, p], targets[i]
        )

    def leg1_relay(s, p):
        block = af.at[s, y, half(p)]
        return remote(block, block, sf1.at[s, p], q1.at[s, p], relay_to[s // 2])

    def leg2(s, i, p):
        block = af.at[s, y, half(p)]
        return remote(block, block, s2.at[s, i, p], q2.at[s, i, p], dev_y[i])

    def leg2_landed(s, i, p):
        block = af.at[s, (y_down, y_up)[i], half(p)]
        return remote(block, block, s2.at[s, i, p], q2.at[s, i, p], dev_y[i])

    def leg2_relay(s, p):
        block = af.at[s, (y_down, y_up)[p], half(p)]
        return remote(block, block, sf2.at[s, p], qf2.at[s, p], dev_y[p])

    def leg2_relay_landed(s, p):
        block = af.at[s, lax.rem(y + 2, 4), half(p)]
        return remote(block, block, sf2.at[s, p], qf2.at[s, p], dev_y[p])

    aligned_source = jnp.logical_and(is_source, offset == 0)
    offset_source = jnp.logical_and(is_source, offset == 1)

    @pl.when(jnp.logical_not(is_source))
    def _():
        leg0(0).start()
        leg0(1).start()

    @pl.when(offset_source)
    def _():
        for p in range(2):
            leg1(0, 0, p).start()
            leg1(0, 1, p).start()

    @pl.when(home)
    def _():
        af[OWN, y] = st[0]

    for j in range(n):
        if j >= EARLY:
            mask_int(j)
        to_a(j).start()
        to_sib(j).start()

    @pl.when(is_source)
    def _():
        for p in range(2):
            leg0(p).wait_recv()
            leg1(1, 0, p).start()
            leg1(1, 1, p).start()

    @pl.when(home)
    def _():
        af[NEAR_X, y] = st[1]

    def spread_z(s):
        for p in range(2):
            def arrive():
                leg1_relay(s, p).wait_recv()

                @pl.when(relays[s // 2])
                def _():
                    leg1_relay(s, p).start()

            if s // 2:
                arrive()
            else:
                pl.when(jnp.logical_not(home))(arrive)
            leg2(s, 0, p).start()
            leg2(s, 1, p).start()

    def spread_y(s):
        for p in range(2):
            leg2_landed(s, p, p).wait_recv()
            leg2_relay(s, p).start()

    def take_amp(s):
        for p in range(2):
            leg2_landed(s, 1 - p, p).wait_recv()
            leg2_relay_landed(s, p).wait_recv()
        for k in range(4):
            c = slice(k * W, (k + 1) * W)
            ah[s, :, c], al[s, :, c] = split(af[s, k])

    loads[4].wait()
    res_rows = mm(onehot((2 * TILE, 32), 0, 2 * row), res_in[...].astype(BF16))
    res_tiles[...] = res_rows.astype(BF16)

    def take_int(j):
        remote(bf.at[kk_a, j], bf.at[kk_a, j], sb.at[j], rb.at[j], sib).wait_recv()
        forward(j).start()
        remote(bf.at[kk_sib, j], bf.at[kk_sib, j], ss.at[j], rs.at[j], sib).wait_recv()
        remote(bf.at[kk_as, j], bf.at[kk_as, j], sf.at[j], rf.at[j], sib).wait_recv()
        for q in range(4):
            r = slice(q * W, (q + 1) * W)
            bh[j, r, :], bl[j, r, :] = split(bf[q, j])

    def multiply(s, j):
        high = bh[j]
        total = mm(ah[s], high) + mm(al[s], high) + mm(ah[s], bl[j])
        part[s, j, 0] = total[:, :HALF]
        part[s, j, 1] = total[:, HALF:]

    def first_x(i, j):
        return remote(part.at[FAR - 2 * i, j, 0], r1x.at[j, i], s1x.at[j, i], q1x.at[j, i], dev_b)

    def first_z(i, j):
        return remote(part.at[FAR - i, j, 1], r1z.at[j, i], s1z.at[j, i], q1z.at[j, i], dev_z)

    def second_z(j):
        return remote(part.at[NEAR_Z, j, 0], r2z.at[j], s2z.at[j], q2z.at[j], dev_z)

    def second_x(j):
        return remote(part.at[NEAR_X, j, 1], r2x.at[j], s2x.at[j], q2x.at[j], dev_b)

    def far(j):
        multiply(FAR, j)
        first_x(0, j).start()
        first_z(0, j).start()

    def near_x(j):
        multiply(NEAR_X, j)
        first_x(1, j).start()

    def near_z(j):
        multiply(NEAR_Z, j)
        first_z(1, j).start()

    def second(j):
        first_x(0, j).wait_recv()
        part[NEAR_Z, j, 0] += r1x[j, 0]
        second_z(j).start()
        first_z(0, j).wait_recv()
        part[NEAR_X, j, 1] += r1z[j, 0]
        second_x(j).start()

    def loop(lo, hi, *steps):
        def body(j, carry):
            for step in steps:
                step(j)
            return carry

        lax.fori_loop(lo, hi, body, 0)

    def start_own():
        @pl.when(aligned_source)
        def _():
            for p in range(2):
                leg1(0, 0, p).start()
                leg1(0, 1, p).start()

    spread_z(NEAR_Z)
    spread_z(FAR)
    spread_y(NEAR_Z)
    spread_z(NEAR_X)
    spread_y(FAR)
    start_own()
    take_amp(NEAR_Z)
    loop(0, BACKLOG, take_int, near_z)
    spread_y(NEAR_X)
    take_amp(FAR)
    loop(0, BACKLOG, far)
    spread_z(OWN)
    take_amp(NEAR_X)
    loop(0, BACKLOG, near_x)
    loop(BACKLOG, LAG, take_int, far, near_z, near_x)
    loop(LAG, 5, take_int, far, near_z, near_x, lambda j: second(j - LAG))
    spread_y(OWN)
    loop(5, n, take_int, far, near_z, near_x, lambda j: second(j - LAG))
    take_amp(OWN)
    loop(0, n - LAG, lambda j: multiply(OWN, j))
    loop(n - LAG, n, second, lambda j: multiply(OWN, j))

    def store(j):
        c = pl.ds(pl.multiple_of(j * W, W), W)
        return pltpu.make_async_copy(out_v.at[:, c], out_ref.at[:, c], s_out.at[j])

    def finish(j):
        tiles = mm(res_tiles[...], onehot((32, W), 1, (W // TILE) * j))
        first_x(1, j).wait_recv()
        second_z(j).wait_recv()
        first_z(1, j).wait_recv()
        second_x(j).wait_recv()
        c = pl.multiple_of(j * W, W)
        left = part[OWN, j, 0] + r1x[j, 1] + r2z[j]
        right = part[OWN, j, 1] + r1z[j, 1] + r2x[j]
        out_v[:, pl.ds(c, HALF)] = left * tiles[:, :HALF]
        out_v[:, pl.ds(c + HALF, HALF)] = right * tiles[:, HALF:]
        store(j).start()

    loop(0, n, finish)

    @pl.when(jnp.logical_not(is_source))
    def _():
        leg0(0).wait_send()
        leg0(1).wait_send()

    @pl.when(is_source)
    def _():
        for b in range(2):
            for i in range(2):
                for p in range(2):
                    leg1(b, i, p).wait_send()

    for s in range(4):
        for p in range(2):
            @pl.when(relays[s // 2])
            def _():
                leg1_relay(s, p).wait_send()

            for i in range(2):
                leg2(s, i, p).wait_send()
            leg2_relay(s, p).wait_send()

    def drain(j):
        to_a(j).wait_send()
        to_sib(j).wait_send()
        forward(j).wait_send()
        for i in range(2):
            first_x(i, j).wait_send()
            first_z(i, j).wait_send()
        second_x(j).wait_send()
        second_z(j).wait_send()
        store(j).wait()

    loop(0, n, drain)


def on_device(amplitudes, integrals, amp_mask, int_mask, res_mask):
    rows, depth = amplitudes.shape
    cols = integrals.shape[1]
    n = cols // W
    dma = pltpu.SemaphoreType.DMA
    vmem = pltpu.VMEM
    return pl.pallas_call(
        kernel,
        out_shape=jax.ShapeDtypeStruct((rows, cols), F32),
        in_specs=[pl.BlockSpec(memory_space=pltpu.HBM)] * 5,
        out_specs=pl.BlockSpec(memory_space=pltpu.HBM),
        scratch_shapes=[
            vmem((rows, depth), F32),
            vmem((depth, cols), F32),
            vmem(amp_mask.shape, jnp.int32),
            vmem(int_mask.shape, jnp.int32),
            vmem(res_mask.shape, jnp.int32),
            vmem((rows, cols), F32),
            vmem((2, rows, depth), F32),
            vmem((4, 4, rows, depth), F32),
            vmem((4, rows, 4 * depth), BF16),
            vmem((4, rows, 4 * depth), BF16),
            vmem((4, n, depth, W), F32),
            vmem((n, 4 * depth, W), BF16),
            vmem((n, 4 * depth, W), BF16),
            vmem((4, n, 2, rows, HALF), F32),
            vmem((n, 2, rows, HALF), F32),
            vmem((n, 2, rows, HALF), F32),
            vmem((n, rows, HALF), F32),
            vmem((n, rows, HALF), F32),
            vmem((rows, 32), BF16),
            vmem((8, 32), F32),
            dma((5,)), dma((n,)), dma((2,)), dma((2,)), dma((2, 2, 2)), dma((4, 2)), dma((4, 2)),
            dma((4, 2, 2)), dma((4, 2, 2)), dma((4, 2)), dma((4, 2)),
            dma((n,)), dma((n,)), dma((n,)), dma((n,)), dma((n,)), dma((n,)),
            dma((n, 2)), dma((n, 2)), dma((n, 2)), dma((n, 2)),
            dma((n,)), dma((n,)), dma((n,)), dma((n,)),
        ],
        compiler_params=pltpu.CompilerParams(
            collective_id=0, has_side_effects=True, vmem_limit_bytes=60 * 2**20
        ),
        cost_estimate=pl.CostEstimate(
            flops=2 * 3 * 4 * rows * 4 * depth * cols,
            bytes_accessed=4 * (rows * depth + depth * cols + rows * cols),
            transcendentals=0,
        ),
        name="ladder",
    )(amplitudes, integrals, amp_mask, int_mask, res_mask)


def solution(mesh):
    placed = (P("row", "col"), P("row", "col"), P(), P("row", "col"), P(None, "col"))
    return jax.shard_map(
        on_device, mesh=mesh, in_specs=placed, out_specs=P("row", "col"), check_vma=False
    )
```

```python
import jax
import jax.numpy as jnp
from jax import lax
from jax.experimental import pallas as pl
from jax.experimental.pallas import tpu as pltpu
from jax.sharding import PartitionSpec as P

TILE = 64
W = 256
HALF = 128
BACKLOG = 1
LAG = 2
EARLY = 4
PIECES = 2
PIECE = 128 // PIECES
OWN, NEAR_X, NEAR_Z, FAR = 0, 1, 2, 3
MESH = pl.DeviceIdType.MESH
F32 = jnp.float32
BF16 = jnp.bfloat16


def device(x, z_lo, core, z_hi, y):
    return (z_lo * 8 + x * 2 + core, z_hi * 4 + y)


def remote(src, dst, send_sem, recv_sem, target):
    return pltpu.make_async_remote_copy(
        src_ref=src, dst_ref=dst, send_sem=send_sem, recv_sem=recv_sem,
        device_id=target, device_id_type=MESH,
    )


def onehot(shape, dim, offset):
    tile = lax.div(lax.broadcasted_iota(jnp.int32, shape, dim), TILE) + offset
    return (tile == lax.broadcasted_iota(jnp.int32, shape, 1 - dim)).astype(BF16)


def mm(a, b):
    return jnp.dot(a, b, preferred_element_type=F32)


def split(value):
    high = value.astype(BF16)
    return high, (value - high.astype(F32)).astype(BF16)


def kernel(
    amp_hbm, int_hbm, amp_mask_hbm, int_mask_hbm, res_mask_hbm, out_ref,
    amp_in, int_in, amp_tiles, int_tiles, res_in,
    st, af, ah, al, bf, bh, bl, part, r1x, r1z, r2x, r2z, res_tiles, mask8,
    s_in, s0, q0, s1, q1, sf1, s2, q2, sf2, qf2,
    sb, rb, ss, rs, sf, rf, s1x, q1x, s1z, q1z, s2x, q2x, s2z, q2z,
):
    n = bf.shape[1]
    loads = [
        pltpu.make_async_copy(src, dst, s_in.at[i])
        for i, (src, dst) in enumerate((
            (amp_hbm, amp_in), (amp_mask_hbm, amp_tiles), (int_mask_hbm, int_tiles),
            (int_hbm, int_in), (res_mask_hbm, res_in),
        ))
    ]
    for load in loads:
        load.start()

    row, col = lax.axis_index("row"), lax.axis_index("col")
    core, x, z = lax.rem(row, 2), lax.rem(lax.div(row, 2), 4), lax.div(row, 8)
    y, h = lax.rem(col, 4), lax.div(col, 4)
    odd = lax.rem(x, 2)
    xa = x + 1 - 2 * odd
    xb = lax.rem(x + 3 + 2 * odd, 4)
    sib = device(x, z, 1 - core, h, y)
    dev_a = device(xa, z, core, h, y)
    dev_b = device(xb, z, core, h, y)
    dev_z = device(x, 1 - z, core, h, y)
    y_up, y_down = lax.rem(y + 1, 4), lax.rem(y + 3, 4)
    dev_y = (device(x, z, core, h, y_up), device(x, z, core, h, y_down))
    kk = 2 * odd + core
    kk_sib = 2 * odd + 1 - core
    kk_a = 2 * (1 - odd) + core
    kk_as = 2 * (1 - odd) + 1 - core

    def at(z_to, h_to):
        return device(x, z_to, core, lax.rem(h_to + 8, 4), y)

    def flag(condition):
        return condition.astype(jnp.int32)

    q = lax.div(x, 2)
    is_source = lax.rem(h, 2) == q
    z_to = lax.div(h, 2)
    offset = lax.rem(z + z_to, 2)
    targets = (
        at(z_to, h + 1 - offset),
        at(z_to, h - (1 - offset) + offset * (1 - 2 * z_to)),
    )
    h_from = 2 * z + q
    place = lax.rem(h - h_from + 4, 4)
    home = place == 0
    relay = 3 - 2 * q
    side = 1 + 2 * z
    relays = (place == relay, jnp.logical_or(home, place == side))
    relay_to = (at(z, h_from + 2), at(z, h_from + 2 + flag(home) * (1 - 2 * z)))
    opposite = place == 2
    from_aligned = at(z, h_from + relay * flag(opposite))
    direct = flag(jnp.logical_or(home, place == side))
    from_offset = at(z + direct * (1 - 2 * z), h_from + side * flag(opposite))

    barrier = pltpu.get_barrier_semaphore()
    for peer in (sib, dev_a, dev_b, dev_z, *dev_y, from_offset):
        pl.semaphore_signal(barrier, inc=1, device_id=peer, device_id_type=MESH)

    @pl.when(jnp.logical_not(home))
    def _():
        pl.semaphore_signal(barrier, inc=1, device_id=from_aligned, device_id_type=MESH)

    for load in loads[:2]:
        load.wait()
    rows = mm(onehot((2 * TILE, 32), 0, 2 * row), amp_tiles[...].astype(BF16)).astype(BF16)
    st[0] = amp_in[...] * mm(rows, onehot((64, W), 1, 4 * col))

    def to_a(j):
        return remote(bf.at[kk, j], bf.at[kk, j], sb.at[j], rb.at[j], dev_a)

    def to_sib(j):
        return remote(bf.at[kk, j], bf.at[kk, j], ss.at[j], rs.at[j], sib)

    def forward(j):
        return remote(bf.at[kk_a, j], bf.at[kk_a, j], sf.at[j], rf.at[j], sib)

    for load in loads[2:4]:
        load.wait()
    mask8[...] = jnp.zeros_like(mask8)
    mask8[0:4, :] = int_tiles[...].astype(F32)
    mask8b = mask8[...].astype(BF16)

    def mask_int(j):
        tiles = mm(mask8b, onehot((32, W), 1, (W // TILE) * j))
        for t in range(4):
            r = slice(t * TILE, (t + 1) * TILE)
            bf[kk, j, r, :] = int_in[r, j * W:(j + 1) * W] * tiles[t:t + 1, :]

    for j in range(EARLY):
        mask_int(j)

    pl.semaphore_wait(barrier, 6 + 2 * flag(is_source) + flag(relays[0]) + flag(relays[1]))

    def piece(p):
        return pl.ds(p * PIECE, PIECE)

    def leg0(p):
        return remote(st.at[0, piece(p)], st.at[1, piece(p)], s0.at[p], q0.at[p], dev_b)

    def leg1(b, i, p):
        s = 2 * offset + b
        return remote(
            st.at[b, piece(p)], af.at[s, y, piece(p)], s1.at[b, i, p], q1.at[s, p], targets[i]
        )

    def leg1_relay(s, p):
        block = af.at[s, y, piece(p)]
        return remote(block, block, sf1.at[s, p], q1.at[s, p], relay_to[s // 2])

    def leg2(s, i, p):
        block = af.at[s, y, piece(p)]
        return remote(block, block, s2.at[s, i, p], q2.at[s, i, p], dev_y[i])

    def leg2_landed(s, i, p):
        block = af.at[s, (y_down, y_up)[i], piece(p)]
        return remote(block, block, s2.at[s, i, p], q2.at[s, i, p], dev_y[i])

    def leg2_relay(s, p):
        way = p // (PIECES // 2)
        block = af.at[s, (y_down, y_up)[way], piece(p)]
        return remote(block, block, sf2.at[s, p], qf2.at[s, p], dev_y[way])

    def leg2_relay_landed(s, p):
        block = af.at[s, lax.rem(y + 2, 4), piece(p)]
        return remote(block, block, sf2.at[s, p], qf2.at[s, p], dev_y[p // (PIECES // 2)])

    aligned_source = jnp.logical_and(is_source, offset == 0)
    offset_source = jnp.logical_and(is_source, offset == 1)

    @pl.when(jnp.logical_not(is_source))
    def _():
        for p in range(PIECES):
            leg0(p).start()

    @pl.when(offset_source)
    def _():
        for p in range(PIECES):
            leg1(0, 0, p).start()
            leg1(0, 1, p).start()

    @pl.when(home)
    def _():
        af[OWN, y] = st[0]

    for j in range(n):
        if j >= EARLY:
            mask_int(j)
        to_a(j).start()
        to_sib(j).start()

    @pl.when(is_source)
    def _():
        for p in range(PIECES):
            leg0(p).wait_recv()
            leg1(1, 0, p).start()
            leg1(1, 1, p).start()

    @pl.when(home)
    def _():
        af[NEAR_X, y] = st[1]

    def spread_z(s):
        for p in range(PIECES):
            def arrive():
                leg1_relay(s, p).wait_recv()

                @pl.when(relays[s // 2])
                def _():
                    leg1_relay(s, p).start()

            if s // 2:
                arrive()
            else:
                pl.when(jnp.logical_not(home))(arrive)
            leg2(s, 0, p).start()
            leg2(s, 1, p).start()

    def spread_y(s):
        for p in range(PIECES):
            leg2_landed(s, p // (PIECES // 2), p).wait_recv()
            leg2_relay(s, p).start()

    def take_amp(s):
        for p in range(PIECES):
            leg2_landed(s, 1 - p // (PIECES // 2), p).wait_recv()
            leg2_relay_landed(s, p).wait_recv()
        for k in range(4):
            c = slice(k * W, (k + 1) * W)
            ah[s, :, c], al[s, :, c] = split(af[s, k])

    loads[4].wait()
    res_rows = mm(onehot((2 * TILE, 32), 0, 2 * row), res_in[...].astype(BF16))
    res_tiles[...] = res_rows.astype(BF16)

    def take_int(j):
        remote(bf.at[kk_a, j], bf.at[kk_a, j], sb.at[j], rb.at[j], sib).wait_recv()
        forward(j).start()
        remote(bf.at[kk_sib, j], bf.at[kk_sib, j], ss.at[j], rs.at[j], sib).wait_recv()
        remote(bf.at[kk_as, j], bf.at[kk_as, j], sf.at[j], rf.at[j], sib).wait_recv()
        for q in range(4):
            r = slice(q * W, (q + 1) * W)
            bh[j, r, :], bl[j, r, :] = split(bf[q, j])

    def multiply(s, j):
        high = bh[j]
        total = mm(ah[s], high) + mm(al[s], high) + mm(ah[s], bl[j])
        part[s, j, 0] = total[:, :HALF]
        part[s, j, 1] = total[:, HALF:]

    def first_x(i, j):
        return remote(part.at[FAR - 2 * i, j, 0], r1x.at[j, i], s1x.at[j, i], q1x.at[j, i], dev_b)

    def first_z(i, j):
        return remote(part.at[FAR - i, j, 1], r1z.at[j, i], s1z.at[j, i], q1z.at[j, i], dev_z)

    def second_z(j):
        return remote(part.at[NEAR_Z, j, 0], r2z.at[j], s2z.at[j], q2z.at[j], dev_z)

    def second_x(j):
        return remote(part.at[NEAR_X, j, 1], r2x.at[j], s2x.at[j], q2x.at[j], dev_b)

    def far(j):
        multiply(FAR, j)
        first_x(0, j).start()
        first_z(0, j).start()

    def near_x(j):
        multiply(NEAR_X, j)
        first_x(1, j).start()

    def near_z(j):
        multiply(NEAR_Z, j)
        first_z(1, j).start()

    def second(j):
        first_x(0, j).wait_recv()
        part[NEAR_Z, j, 0] += r1x[j, 0]
        second_z(j).start()
        first_z(0, j).wait_recv()
        part[NEAR_X, j, 1] += r1z[j, 0]
        second_x(j).start()

    def loop(lo, hi, *steps):
        def body(j, carry):
            for step in steps:
                step(j)
            return carry

        lax.fori_loop(lo, hi, body, 0)

    def start_own():
        @pl.when(aligned_source)
        def _():
            for p in range(PIECES):
                leg1(0, 0, p).start()
                leg1(0, 1, p).start()

    spread_z(NEAR_Z)
    spread_z(FAR)
    spread_y(NEAR_Z)
    spread_z(NEAR_X)
    spread_y(FAR)
    start_own()
    take_amp(NEAR_Z)
    loop(0, BACKLOG, take_int, near_z)
    spread_y(NEAR_X)
    take_amp(FAR)
    loop(0, BACKLOG, far)
    spread_z(OWN)
    take_amp(NEAR_X)
    loop(0, BACKLOG, near_x)
    loop(BACKLOG, LAG, take_int, far, near_z, near_x)
    loop(LAG, 5, take_int, far, near_z, near_x, lambda j: second(j - LAG))
    spread_y(OWN)
    loop(5, n, take_int, far, near_z, near_x, lambda j: second(j - LAG))
    take_amp(OWN)
    loop(0, n - LAG, lambda j: multiply(OWN, j))
    loop(n - LAG, n, second, lambda j: multiply(OWN, j))

    def finish(j):
        tiles = mm(res_tiles[...], onehot((32, W), 1, (W // TILE) * j))
        first_x(1, j).wait_recv()
        second_z(j).wait_recv()
        first_z(1, j).wait_recv()
        second_x(j).wait_recv()
        c = pl.multiple_of(j * W, W)
        left = part[OWN, j, 0] + r1x[j, 1] + r2z[j]
        right = part[OWN, j, 1] + r1z[j, 1] + r2x[j]
        out_ref[:, pl.ds(c, HALF)] = left * tiles[:, :HALF]
        out_ref[:, pl.ds(c + HALF, HALF)] = right * tiles[:, HALF:]

    loop(0, n, finish)

    @pl.when(jnp.logical_not(is_source))
    def _():
        for p in range(PIECES):
            leg0(p).wait_send()

    @pl.when(is_source)
    def _():
        for b in range(2):
            for i in range(2):
                for p in range(PIECES):
                    leg1(b, i, p).wait_send()

    for s in range(4):
        for p in range(PIECES):
            @pl.when(relays[s // 2])
            def _():
                leg1_relay(s, p).wait_send()

            for i in range(2):
                leg2(s, i, p).wait_send()
            leg2_relay(s, p).wait_send()

    def drain(j):
        to_a(j).wait_send()
        to_sib(j).wait_send()
        forward(j).wait_send()
        for i in range(2):
            first_x(i, j).wait_send()
            first_z(i, j).wait_send()
        second_x(j).wait_send()
        second_z(j).wait_send()

    loop(0, n, drain)


def on_device(amplitudes, integrals, amp_mask, int_mask, res_mask):
    rows, depth = amplitudes.shape
    cols = integrals.shape[1]
    n = cols // W
    dma = pltpu.SemaphoreType.DMA
    vmem = pltpu.VMEM
    return pl.pallas_call(
        kernel,
        out_shape=pltpu.VMEM((rows, cols), F32),
        in_specs=[pl.BlockSpec(memory_space=pltpu.HBM)] * 5,
        out_specs=pl.BlockSpec(memory_space=pltpu.VMEM),
        scratch_shapes=[
            vmem((rows, depth), F32),
            vmem((depth, cols), F32),
            vmem(amp_mask.shape, jnp.int32),
            vmem(int_mask.shape, jnp.int32),
            vmem(res_mask.shape, jnp.int32),
            vmem((2, rows, depth), F32),
            vmem((4, 4, rows, depth), F32),
            vmem((4, rows, 4 * depth), BF16),
            vmem((4, rows, 4 * depth), BF16),
            vmem((4, n, depth, W), F32),
            vmem((n, 4 * depth, W), BF16),
            vmem((n, 4 * depth, W), BF16),
            vmem((4, n, 2, rows, HALF), F32),
            vmem((n, 2, rows, HALF), F32),
            vmem((n, 2, rows, HALF), F32),
            vmem((n, rows, HALF), F32),
            vmem((n, rows, HALF), F32),
            vmem((rows, 32), BF16),
            vmem((8, 32), F32),
            dma((5,)), dma((PIECES,)), dma((PIECES,)),
            dma((2, 2, PIECES)), dma((4, PIECES)), dma((4, PIECES)),
            dma((4, 2, PIECES)), dma((4, 2, PIECES)), dma((4, PIECES)), dma((4, PIECES)),
            dma((n,)), dma((n,)), dma((n,)), dma((n,)), dma((n,)), dma((n,)),
            dma((n, 2)), dma((n, 2)), dma((n, 2)), dma((n, 2)),
            dma((n,)), dma((n,)), dma((n,)), dma((n,)),
        ],
        compiler_params=pltpu.CompilerParams(
            collective_id=0, has_side_effects=True, vmem_limit_bytes=56 * 2**20
        ),
        cost_estimate=pl.CostEstimate(
            flops=2 * 3 * 4 * rows * 4 * depth * cols,
            bytes_accessed=4 * (rows * depth + depth * cols + rows * cols),
            transcendentals=0,
        ),
        name="ladder",
    )(*(
        pltpu.with_memory_space_constraint(a, pltpu.HBM)
        for a in (amplitudes, integrals, amp_mask, int_mask, res_mask)
    ))


def solution(mesh):
    placed = (P("row", "col"), P("row", "col"), P(), P("row", "col"), P(None, "col"))
    return jax.shard_map(
        on_device, mesh=mesh, in_specs=placed, out_specs=P("row", "col"), check_vma=False
    )
```
